256 devices in a mesh: batch: 32 (over y, x, core), leaf: 8 (over z).
Axes of the slice: x: 4, y: 4, z: 8, core: 2. Of those that a mesh axis runs over, the one named last changes fastest.
Arguments:
- queries: bfloat16 [32, 1024, 4096], P('batch', 'leaf'), may hold values from -6 to 6
- keys: bfloat16 [32, 1024, 512], P('batch', 'leaf'), may hold values from -6 to 6
- values: bfloat16 [32, 1024, 512], P('batch', 'leaf'), may hold values from -6 to 6
- out_grad: bfloat16 [32, 1024, 4096], P('batch', 'leaf'), may hold values from -6 to 6
- inputs: bfloat16 [32, 1024, 5120], P('batch', 'leaf'), may hold values from -6 to 6
- parents: int32 [32, 8], P('batch'), may hold values from 0 to 6, as said below
- lengths: int32 [32, 8], P('batch'), may hold values from 16 to 128, as said below
Outputs:
- query_grad: bfloat16 [32, 1024, 4096], P('batch', 'leaf')
- key_grad: bfloat16 [32, 1024, 512], P('batch', 'leaf')
- value_grad: bfloat16 [32, 1024, 512], P('batch', 'leaf')
- weight_grad: float32 [5120, 512], P(('batch', 'leaf'))
The draws below stay inside these ranges and needn't reach their ends.
Inputs may be any that keep to these rules, and one draw needn't show every extreme that they name: parents[t, 0] = 0 and parents[t, s] < s for s >= 1. `lengths`: segment 0 of every tree holds 128 live tokens; the others at least 16.
All inputs are finite; a program needn't handle non-finite values.
Results may differ from the reference program's by a relative error of at most 0.015.
Values may be sent and summed in bfloat16 or wider, within the bound.
No kernel may reach another device: no remote copies, remote signals or barrier semaphores. Data moves between devices by JAX's collectives and lax.ppermute only.
A program may use at most 128 MiB of HBM per device.

```python
import math
import jax
import jax.numpy as jnp
from jax import lax

D = 5120
HQ = 32
HD = 128
TOK_DEV = 128
NODES = 8
TREES = 32
ROWS = 1024
KVW = 512


def draw_queries(key, part):
    key = jax.random.fold_in(key, 11)
    shape = (TREES, ROWS, HQ * HD)
    base = jax.random.normal(key, shape, jnp.float32)
    return jnp.clip(base, -6.0, 6.0).astype(jnp.bfloat16)


def draw_keys(key, part):
    key = jax.random.fold_in(key, 13)
    shape = (TREES, ROWS, KVW)
    base = jax.random.normal(key, shape, jnp.float32)
    return jnp.clip(base, -6.0, 6.0).astype(jnp.bfloat16)


def draw_parents(key, part):
    key = jax.random.fold_in(key, 5)
    node_ids = jnp.arange(NODES, dtype=jnp.int32)
    tree_ids = jnp.arange(TREES, dtype=jnp.int32)
    raw = jax.random.randint(key, (TREES, NODES), 0, 1 << 20, dtype=jnp.int32)
    drawn = raw % jnp.maximum(node_ids, 1)[None, :]
    last_case = (tree_ids[:, None] == 0) & (node_ids[None, :] == NODES - 1)
    return jnp.where(last_case, jnp.maximum(NODES - 2, 0), drawn).astype(jnp.int32)


def draw_lengths(key, part):
    key = jax.random.fold_in(key, 7)
    node_ids = jnp.arange(NODES, dtype=jnp.int32)
    raw = jax.random.randint(key, (TREES, NODES), TOK_DEV // 8, TOK_DEV + 1, dtype=jnp.int32)
    return jnp.where(node_ids[None, :] == 0, TOK_DEV, raw).astype(jnp.int32)


def spiked(values, key, source, target, parts, factor):
    owner, partner = [(jnp.arange(values.shape[axis_at]) // (values.shape[axis_at] // parts)).reshape([-1 if axis == axis_at else 1 for axis in range(values.ndim)]) for axis_at in (source, target)]
    chosen = jax.random.permutation(key, parts)[partner]
    strong = (owner == chosen) | (owner == (partner + parts // 2) % parts)
    return jnp.where(strong, factor * values, values)


def level_of(key, dims, shards, smallest, high):
    def one(dim, parts):
        draws = jax.random.uniform(jax.random.fold_in(jax.random.fold_in(key, 6), dim), (parts,), jnp.float32, smallest / len(shards), high / len(shards))
        return jnp.repeat(jnp.exp(draws), dims[dim] // parts).reshape((-1,) + (1,) * (len(dims) - dim - 1))

    factor_of = one(*shards[0])
    for cut in shards[1:]:
        factor_of = factor_of * one(*cut)
    return factor_of


def noise(rng, dims, deviation, most, shards=(), kind=jnp.bfloat16):
    values = jax.random.normal(rng, dims, jnp.float32) * deviation
    if len(shards) > 0:
        values = level_of(rng, dims, shards, -0.22, 0.18) * values
    return jnp.clip(values, min=-most, max=most).astype(kind)


def noise_with(key, shape, deviation, most, shards, heavy, kind=jnp.bfloat16):
    array = deviation * jax.random.normal(key, shape, jnp.float32)
    if shards:
        array = array * level_of(key, shape, shards, -0.22, 0.18)
    return jnp.clip(spiked(array, jax.random.fold_in(key, 3), *heavy), -most, most).astype(kind)


def setup_inputs(seed: int = 0) -> dict:
    seeds = jax.random.split(jax.random.key(seed), 8)
    queries = draw_queries(jax.random.fold_in(seeds[7], 71), 0)
    keys = draw_keys(jax.random.fold_in(seeds[7], 71), 0)
    values = noise(seeds[2], (TREES, ROWS, KVW), 1.0, 6.0, ((0, 32), (1, 8)))
    out_grad = noise(seeds[3], (TREES, ROWS, HQ * HD), 1.0, 6.0, ((0, 32), (1, 8)))
    inputs = noise_with(seeds[4], (TREES, ROWS, D), 1.0, 6.0, ((0, 32), (1, 8)), (1, 2, 8, 2.0))
    parents = draw_parents(jax.random.fold_in(seeds[7], 71), 0)
    lengths = draw_lengths(jax.random.fold_in(seeds[7], 71), 0)
    return dict(queries=queries, keys=keys, values=values, out_grad=out_grad, inputs=inputs, parents=parents, lengths=lengths)


def lineage_table(parent_row):
    node_count = parent_row.shape[0]
    node_ids = jnp.arange(node_count, dtype=jnp.int32)
    cursor = node_ids
    table = node_ids[:, None] == node_ids[None, :]
    for _ in range(node_count):
        cursor = parent_row[cursor].astype(jnp.int32)
        table = table | (cursor[:, None] == node_ids[None, :])
    return table

def tree_grads(query_tree, key_tree, value_tree, grad_tree, parent_row, length_row):
    total_rows = query_tree.shape[0]
    node_count = parent_row.shape[0]
    segment = total_rows // node_count
    kv_width = key_tree.shape[1]
    heads_kv = kv_width // HD
    group_size = query_tree.shape[1] // kv_width
    table = lineage_table(parent_row)
    node_of = jnp.arange(total_rows, dtype=jnp.int32) // segment
    place = jnp.arange(total_rows, dtype=jnp.int32) % segment
    row_length = length_row[node_of]
    same_node = node_of[:, None] == node_of[None, :]
    lineage = table[node_of][:, node_of]
    above = lineage & ~same_node & (place[None, :] < row_length[None, :])
    allowed = above | same_node & (place[None, :] <= place[:, None])
    live = place < row_length
    masked_grad = jnp.where(live[:, None], grad_tree, jnp.zeros_like(grad_tree))
    query_four = query_tree.astype(jnp.float32).reshape(total_rows, heads_kv, group_size, HD)
    grad_four = masked_grad.astype(jnp.float32).reshape(total_rows, heads_kv, group_size, HD)
    key_three = key_tree.astype(jnp.float32).reshape(total_rows, heads_kv, HD)
    value_three = value_tree.astype(jnp.float32).reshape(total_rows, heads_kv, HD)
    score_scale = 1.0 / math.sqrt(HD)
    scores = jnp.einsum('ikgd,jkd->kgij', query_four, key_three) * score_scale
    scores = jnp.where(allowed, scores, -jnp.inf)
    row_max = lax.optimization_barrier(jnp.max(scores, axis=-1, keepdims=True))
    raised = jnp.exp(scores - row_max)
    probs = raised / lax.optimization_barrier(jnp.sum(raised, axis=-1, keepdims=True))
    probs_low = probs.astype(jnp.bfloat16)
    dprobs = jnp.einsum('ikgd,jkd->kgij', grad_four, value_three)
    delta = lax.optimization_barrier(jnp.sum(probs * dprobs, axis=-1, keepdims=True))
    dscores_low = (probs * (dprobs - delta)).astype(jnp.bfloat16)
    dscore_wide = dscores_low.astype(jnp.float32)
    query_grad = jnp.einsum('kgij,jkd->ikgd', dscore_wide, key_three) * score_scale
    key_grad = jnp.einsum('kgij,ikgd->jkd', dscore_wide, query_four) * score_scale
    value_grad = jnp.einsum('kgij,ikgd->jkd', probs_low.astype(jnp.float32), grad_four)
    return (query_grad.reshape(total_rows, -1).astype(jnp.bfloat16), key_grad.reshape(total_rows, -1).astype(jnp.bfloat16), value_grad.reshape(total_rows, -1).astype(jnp.bfloat16))

def reference(queries, keys, values, out_grad, inputs, parents, lengths):

    def one_tree(carry, items):
        query_tree, key_tree, value_tree, grad_tree, input_tree, parent_row, length_row = items
        query_grad, key_grad, value_grad = tree_grads(query_tree, key_tree, value_tree, grad_tree, parent_row, length_row)
        carry = carry + jnp.dot(input_tree.T, value_grad, preferred_element_type=jnp.float32)
        return (carry, (query_grad, key_grad, value_grad))
    start_sum = jnp.zeros((inputs.shape[2], keys.shape[2]), jnp.float32)
    weight_grad, outputs = lax.scan(one_tree, start_sum, (queries, keys, values, out_grad, inputs, parents, lengths))
    return (outputs[0], outputs[1], outputs[2], weight_grad)
```

```python
import math

import jax
import jax.numpy as jnp
from jax import lax
from jax.experimental import pallas as pl
from jax.experimental.pallas import tpu as pltpu
from jax.sharding import Mesh
from jax.sharding import PartitionSpec as P

HD = 128
NEG = -1e30
F32 = jnp.float32
BF16 = jnp.bfloat16
NT = (((1,), (1,)), ((), ()))
TN = (((0,), (0,)), ((), ()))


def attention_kernel(
    own_ref, par_ref, len_ref, q_ref, g_ref, k_ref, v_ref, dq_ref, dk_ref, dv_ref,
    qs, gs, s_scr, dp_scr, p_low, ds_low, m_scr, l_scr, t_scr, dqt, slot_ref, lim_ref,
):
    seg = q_ref.shape[0]
    group = q_ref.shape[1] // HD
    nodes = k_ref.shape[0] // seg
    width = group * seg
    chunk = 2 * seg
    chunks = width // chunk
    scale = 1.0 / math.sqrt(HD)
    own = own_ref[0]

    cursor = own
    slot_ref[0] = own
    lim_ref[0] = seg
    count = jnp.int32(1)
    for step in range(1, nodes):
        more = cursor > 0
        up = jnp.where(more, par_ref[cursor], 0)
        slot_ref[step] = up
        lim_ref[step] = jnp.where(more, len_ref[up], 0)
        count = count + more.astype(jnp.int32)
        cursor = up
    pairs = (count + 1) // 2

    live = lax.broadcasted_iota(jnp.int32, (seg, HD), 0) < len_ref[own]
    for head in range(group):
        qs[head * seg : (head + 1) * seg, :] = q_ref[:, head * HD : (head + 1) * HD]
        gs[head * seg : (head + 1) * seg, :] = jnp.where(
            live, g_ref[:, head * HD : (head + 1) * HD], jnp.zeros((), BF16)
        )

    dk_ref[...] = jnp.zeros_like(dk_ref)
    dv_ref[...] = jnp.zeros_like(dv_ref)
    m_scr[...] = jnp.full_like(m_scr, NEG)
    l_scr[...] = jnp.zeros_like(l_scr)
    t_scr[...] = jnp.zeros_like(t_scr)
    dqt[...] = jnp.zeros_like(dqt)

    def rows_of(ref, p):
        first = pl.multiple_of(slot_ref[2 * p] * seg, seg)
        second = pl.multiple_of(slot_ref[2 * p + 1] * seg, seg)
        return jnp.concatenate([ref[pl.ds(first, seg), :], ref[pl.ds(second, seg), :]], axis=0)

    key_place = lax.broadcasted_iota(jnp.int32, (seg, chunk), 0)
    query_place = lax.broadcasted_iota(jnp.int32, (1, chunk), 1) % seg

    def score_step(p, carry):
        k2 = rows_of(k_ref, p)
        last0 = jnp.where(p == 0, query_place, lim_ref[2 * p] - 1)
        last1 = jnp.broadcast_to(lim_ref[2 * p + 1] - 1, query_place.shape)
        for c in range(chunks):
            cols = slice(c * chunk, (c + 1) * chunk)
            s = lax.dot_general(k2, qs[cols, :], NT, preferred_element_type=F32)
            s0 = jnp.where(key_place <= last0, s[:seg], NEG)
            s1 = jnp.where(key_place <= last1, s[seg:], NEG)
            s_scr[p, :seg, cols] = s0
            s_scr[p, seg:, cols] = s1
            top = jnp.max(jnp.maximum(s0, s1), axis=0, keepdims=True)
            m_scr[:, cols] = jnp.maximum(m_scr[:, cols], top)
        return carry

    lax.fori_loop(0, pairs, score_step, 0)
    rate = scale * math.log2(math.e)

    def prob_step(p, carry):
        v2 = rows_of(v_ref, p)
        for c in range(chunks):
            cols = slice(c * chunk, (c + 1) * chunk)
            e = jnp.exp2((s_scr[p, :, cols] - m_scr[:, cols]) * rate)
            dp = lax.dot_general(v2, gs[cols, :], NT, preferred_element_type=F32)
            s_scr[p, :, cols] = e
            dp_scr[p, :, cols] = dp
            l_scr[:, cols] = l_scr[:, cols] + jnp.sum(e, axis=0, keepdims=True)
            t_scr[:, cols] = t_scr[:, cols] + jnp.sum(e * dp, axis=0, keepdims=True)
        return carry

    lax.fori_loop(0, pairs, prob_step, 0)
    l_scr[...] = 1.0 / l_scr[...]
    t_scr[...] = t_scr[...] * l_scr[...]

    def grad_step(p, carry):
        k2 = rows_of(k_ref, p)
        for c in range(chunks):
            cols = slice(c * chunk, (c + 1) * chunk)
            prob = s_scr[p, :, cols] * l_scr[:, cols]
            p_low[:, cols] = prob.astype(BF16)
            ds = (prob * (dp_scr[p, :, cols] - t_scr[:, cols])).astype(BF16)
            ds_low[:, cols] = ds
            dqt[:, cols] = dqt[:, cols] + lax.dot_general(k2, ds, TN, preferred_element_type=F32)
        dv = jnp.dot(p_low[...], gs[...], preferred_element_type=F32).astype(BF16)
        dk = (jnp.dot(ds_low[...], qs[...], preferred_element_type=F32) * scale).astype(BF16)
        first = pl.multiple_of(slot_ref[2 * p] * seg, seg)
        dv_ref[pl.ds(first, seg), :] = dv[:seg]
        dk_ref[pl.ds(first, seg), :] = dk[:seg]

        @pl.when(2 * p + 1 < count)
        def _():
            second = pl.multiple_of(slot_ref[2 * p + 1] * seg, seg)
            dv_ref[pl.ds(second, seg), :] = dv[seg:]
            dk_ref[pl.ds(second, seg), :] = dk[seg:]

        return carry

    lax.fori_loop(0, pairs, grad_step, 0)
    for head in range(group):
        block = dqt[:, head * seg : (head + 1) * seg] * scale
        dq_ref[:, head * HD : (head + 1) * HD] = block.T.astype(BF16)


def attention(own, parents, lengths, queries, out_grad, kv_all):
    seg, q_width = queries.shape
    rows, kv_width = kv_all.shape[0], kv_all.shape[1] // 2
    heads_kv = kv_width // HD
    per_head = q_width // heads_kv
    nodes = rows // seg
    width = (per_head // HD) * seg
    spec_q = pl.BlockSpec((seg, per_head), lambda k, *_: (0, k))
    spec_k = pl.BlockSpec((rows, HD), lambda k, *_: (0, k))
    spec_v = pl.BlockSpec((rows, HD), lambda k, *_: (0, k + heads_kv))
    pairs = nodes // 2
    return pl.pallas_call(
        attention_kernel,
        out_shape=(
            jax.ShapeDtypeStruct((seg, q_width), BF16),
            jax.ShapeDtypeStruct((rows, kv_width), BF16),
            jax.ShapeDtypeStruct((rows, kv_width), BF16),
        ),
        grid_spec=pltpu.PrefetchScalarGridSpec(
            num_scalar_prefetch=3,
            grid=(heads_kv,),
            in_specs=[spec_q, spec_q, spec_k, spec_v],
            out_specs=[spec_q, spec_k, spec_k],
            scratch_shapes=[
                pltpu.VMEM((width, HD), BF16),
                pltpu.VMEM((width, HD), BF16),
                pltpu.VMEM((pairs, 2 * seg, width), F32),
                pltpu.VMEM((pairs, 2 * seg, width), F32),
                pltpu.VMEM((2 * seg, width), BF16),
                pltpu.VMEM((2 * seg, width), BF16),
                pltpu.VMEM((1, width), F32),
                pltpu.VMEM((1, width), F32),
                pltpu.VMEM((1, width), F32),
                pltpu.VMEM((HD, width), F32),
                pltpu.SMEM((nodes,), jnp.int32),
                pltpu.SMEM((nodes,), jnp.int32),
            ],
        ),
        compiler_params=pltpu.CompilerParams(vmem_limit_bytes=40 * 1024 * 1024),
        cost_estimate=pl.CostEstimate(
            flops=10 * seg * rows * q_width, bytes_accessed=8 * seg * q_width, transcendentals=0
        ),
    )(own, parents, lengths, queries, out_grad, kv_all, kv_all)


def weight_kernel(x_ref, v_ref, out_ref):
    trees = x_ref.shape[0]
    parts = out_ref.shape[0]
    rows = out_ref.shape[1]
    for part in range(parts):
        total = None
        for tree in range(0, trees, 2):
            x2 = jnp.concatenate(
                [
                    x_ref[tree, part * rows : (part + 1) * rows, :],
                    x_ref[tree + 1, part * rows : (part + 1) * rows, :],
                ],
                axis=1,
            )
            v2 = jnp.concatenate([v_ref[tree], v_ref[tree + 1]], axis=0)
            term = jnp.dot(x2, v2, preferred_element_type=F32)
            total = term if total is None else total + term
        out_ref[part] = total.astype(BF16)


def on_device(queries, keys, values, out_grad, inputs, parents, lengths):
    ny, nx, nc = lax.axis_size("y"), lax.axis_size("x"), lax.axis_size("core")
    nz = lax.axis_size("leaf")
    seg, features = inputs.shape[1:]
    kv_width = keys.shape[2]
    own = lax.axis_index("leaf").astype(jnp.int32).reshape(1)

    kv_all = lax.all_gather(
        jnp.concatenate([keys[0], values[0]], axis=1), "leaf", axis=0, tiled=True
    )

    group = nx * nc
    owned = features // (ny * group)
    turned = inputs[0].T.reshape(ny, group, owned, seg).transpose(1, 0, 2, 3)
    turned = turned.reshape(group, ny * owned, seg)
    turned = lax.all_to_all(turned, ("x", "core"), 0, 0, tiled=True)
    kv_all, turned = lax.optimization_barrier((kv_all, turned))

    query_grad, key_part, value_part = attention(
        own, parents[0], lengths[0], queries[0], out_grad[0], kv_all
    )
    value_grad = lax.psum_scatter(value_part, "leaf", scatter_dimension=0, tiled=True)
    key_part, value_grad = lax.optimization_barrier((key_part, value_grad))
    key_grad = lax.psum_scatter(key_part, "leaf", scatter_dimension=0, tiled=True)

    line = lax.all_gather(value_grad, "x", axis=0)
    both = lax.all_gather(line, "core", axis=1).reshape(group, seg, kv_width)
    term = pl.pallas_call(
        weight_kernel,
        out_shape=jax.ShapeDtypeStruct((ny, owned, kv_width), BF16),
        compiler_params=pltpu.CompilerParams(vmem_limit_bytes=40 * 1024 * 1024),
        cost_estimate=pl.CostEstimate(
            flops=2 * features * seg * kv_width, bytes_accessed=4 * features * seg, transcendentals=0
        ),
    )(turned, both)
    term = lax.all_to_all(term, "y", 0, 0, tiled=True)
    term = jnp.sum(term.astype(F32), axis=0).astype(BF16)
    term = lax.all_to_all(term.reshape(nz, owned // nz, kv_width), "leaf", 0, 0, tiled=True)
    weight_grad = jnp.sum(term.astype(F32), axis=0)
    return (query_grad[None], key_grad[None], value_grad[None], weight_grad)


def solution(mesh):
    trees, nodes = mesh.devices.shape
    side = math.isqrt(trees // 2)
    fine = Mesh(mesh.devices.reshape(side, side, 2, nodes), ("y", "x", "core", "leaf"))
    batch = ("y", "x", "core")
    rows = P(batch, "leaf", None)
    return jax.shard_map(
        on_device,
        mesh=fine,
        in_specs=(rows, rows, rows, rows, rows, P(batch, None), P(batch, None)),
        out_specs=(rows, rows, rows, P((*batch, "leaf"), None)),
        check_vma=False,
    )
```

```python
import functools
import math

import jax
import jax.numpy as jnp
from jax import lax
from jax.experimental import pallas as pl
from jax.experimental.pallas import tpu as pltpu
from jax.sharding import Mesh
from jax.sharding import PartitionSpec as P

HD = 128
NEG = -1e30
F32 = jnp.float32
BF16 = jnp.bfloat16
NT = (((1,), (1,)), ((), ()))
TN = (((0,), (0,)), ((), ()))
SCALE = 1.0 / math.sqrt(HD)
RATE = SCALE * math.log2(math.e)
LIMIT = pltpu.CompilerParams(vmem_limit_bytes=60 * 1024 * 1024)


def climb(own_ref, par_ref, len_ref, slot_ref, lim_ref, seg, nodes):
    cursor = own_ref[0]
    slot_ref[0] = cursor
    lim_ref[0] = seg
    count = jnp.int32(1)
    for step in range(1, nodes):
        more = cursor > 0
        up = jnp.where(more, par_ref[cursor], 0)
        slot_ref[step] = up
        lim_ref[step] = jnp.where(more, len_ref[up], 0)
        count = count + more.astype(jnp.int32)
        cursor = up
    return count


def stack_heads(q_ref, g_ref, qs, gs, length):
    seg = q_ref.shape[0]
    live = lax.broadcasted_iota(jnp.int32, (seg, HD), 0) < length
    for head in range(q_ref.shape[1] // HD):
        rows, cols = slice(head * seg, (head + 1) * seg), slice(head * HD, (head + 1) * HD)
        qs[rows, :] = q_ref[:, cols]
        gs[rows, :] = jnp.where(live, g_ref[:, cols], jnp.zeros((), BF16))


def last_places(lim_ref, p, seg, chunk):
    query_place = lax.broadcasted_iota(jnp.int32, (1, chunk), 1) % seg
    last0 = jnp.where(p == 0, query_place, lim_ref[2 * p] - 1)
    last1 = jnp.broadcast_to(lim_ref[2 * p + 1] - 1, query_place.shape)
    return last0, last1


def masked_scores(k2, q, last0, last1):
    seg = k2.shape[0] // 2
    place = lax.broadcasted_iota(jnp.int32, (seg, q.shape[0]), 0)
    s = lax.dot_general(k2, q, NT, preferred_element_type=F32)
    return jnp.where(place <= last0, s[:seg], NEG), jnp.where(place <= last1, s[seg:], NEG)


def value_kernel(own_ref, par_ref, len_ref, q_ref, g_ref, *refs):
    nodes = (len(refs) - 10) // 2
    keys, values = refs[:nodes], refs[nodes : 2 * nodes]
    m_ref, l_ref, qs, gs, kc, dvc, s_scr, p_low, slot_ref, lim_ref = refs[2 * nodes :]
    seg = q_ref.shape[0]
    width = qs.shape[0]
    chunk = 2 * seg
    own = own_ref[0]
    count = climb(own_ref, par_ref, len_ref, slot_ref, lim_ref, seg, nodes)
    pairs = (count + 1) // 2
    stack_heads(q_ref, g_ref, qs, gs, len_ref[own])
    for back in range(nodes):
        kc[back] = keys[back][...]
    dvc[...] = jnp.zeros_like(dvc)
    m_ref[...] = jnp.full_like(m_ref, NEG)
    l_ref[...] = jnp.zeros_like(l_ref)

    def score_step(p, carry):
        k2 = jnp.concatenate([kc[own - slot_ref[2 * p]], kc[own - slot_ref[2 * p + 1]]], axis=0)
        last0, last1 = last_places(lim_ref, p, seg, chunk)
        for c in range(width // chunk):
            cols = slice(c * chunk, (c + 1) * chunk)
            s0, s1 = masked_scores(k2, qs[cols, :], last0, last1)
            s_scr[p, :seg, cols] = s0
            s_scr[p, seg:, cols] = s1
            top = jnp.max(jnp.maximum(s0, s1), axis=0, keepdims=True)
            m_ref[0, :, cols] = jnp.maximum(m_ref[0, :, cols], top)
        return carry

    lax.fori_loop(0, pairs, score_step, 0)

    def sum_step(p, carry):
        for c in range(width // chunk):
            cols = slice(c * chunk, (c + 1) * chunk)
            e = jnp.exp2((s_scr[p, :, cols] - m_ref[0, :, cols]) * RATE)
            s_scr[p, :, cols] = e
            l_ref[0, :, cols] = l_ref[0, :, cols] + jnp.sum(e, axis=0, keepdims=True)
        return carry

    lax.fori_loop(0, pairs, sum_step, 0)
    l_ref[...] = 1.0 / l_ref[...]

    def value_step(p, carry):
        for c in range(width // chunk):
            cols = slice(c * chunk, (c + 1) * chunk)
            p_low[:, cols] = (s_scr[p, :, cols] * l_ref[0, :, cols]).astype(BF16)
        dv = jnp.dot(p_low[...], gs[...], preferred_element_type=F32).astype(BF16)
        dvc[own - slot_ref[2 * p]] = dv[:seg]

        @pl.when(2 * p + 1 < count)
        def _():
            dvc[own - slot_ref[2 * p + 1]] = dv[seg:]

        return carry

    lax.fori_loop(0, pairs, value_step, 0)
    for back in range(nodes):
        values[back][...] = dvc[back]


def score_kernel(kept, own_ref, par_ref, len_ref, q_ref, g_ref, m_ref, l_ref, *refs):
    nodes = len(refs) - 13 - kept
    keys = refs[:nodes]
    v_ref = refs[nodes]
    dq_ref, dk_ref, qs, gs, kc, s_scr, dp_scr, ds_low, t_scr, dqt, slot_ref, lim_ref = refs[nodes + 1 + kept :]
    seg = q_ref.shape[0]
    width = qs.shape[0]
    chunk = 2 * seg
    own = own_ref[0]
    count = climb(own_ref, par_ref, len_ref, slot_ref, lim_ref, seg, nodes)
    pairs = (count + 1) // 2
    stack_heads(q_ref, g_ref, qs, gs, len_ref[own])
    for back in range(nodes):
        kc[back] = keys[back][...]
    dk_ref[...] = jnp.zeros_like(dk_ref)
    t_scr[...] = jnp.zeros_like(t_scr)
    dqt[...] = jnp.zeros_like(dqt)

    def rows(slot):
        return pl.ds(pl.multiple_of(slot_ref[slot] * seg, seg), seg)

    def prob_step(p, carry):
        k2 = jnp.concatenate([kc[own - slot_ref[2 * p]], kc[own - slot_ref[2 * p + 1]]], axis=0)
        v2 = jnp.concatenate([v_ref[rows(2 * p), :], v_ref[rows(2 * p + 1), :]], axis=0)
        last0, last1 = last_places(lim_ref, p, seg, chunk)
        for c in range(width // chunk):
            cols = slice(c * chunk, (c + 1) * chunk)
            s0, s1 = masked_scores(k2, qs[cols, :], last0, last1)
            s = jnp.concatenate([s0, s1], axis=0)
            prob = jnp.exp2((s - m_ref[0, :, cols]) * RATE) * l_ref[0, :, cols]
            dp = lax.dot_general(v2, gs[cols, :], NT, preferred_element_type=F32)
            s_scr[p, :, cols] = prob
            dp_scr[p, :, cols] = dp
            t_scr[:, cols] = t_scr[:, cols] + jnp.sum(prob * dp, axis=0, keepdims=True)
        return carry

    lax.fori_loop(0, pairs, prob_step, 0)

    def grad_step(p, carry):
        k2 = jnp.concatenate([kc[own - slot_ref[2 * p]], kc[own - slot_ref[2 * p + 1]]], axis=0)
        for c in range(width // chunk):
            cols = slice(c * chunk, (c + 1) * chunk)
            ds = (s_scr[p, :, cols] * (dp_scr[p, :, cols] - t_scr[:, cols])).astype(BF16)
            ds_low[:, cols] = ds
            dqt[:, cols] = dqt[:, cols] + lax.dot_general(k2, ds, TN, preferred_element_type=F32)
        dk = (jnp.dot(ds_low[...], qs[...], preferred_element_type=F32) * SCALE).astype(BF16)
        dk_ref[rows(2 * p), :] = dk[:seg]

        @pl.when(2 * p + 1 < count)
        def _():
            dk_ref[rows(2 * p + 1), :] = dk[seg:]

        return carry

    lax.fori_loop(0, pairs, grad_step, 0)
    for head in range(width // seg):
        block = dqt[:, head * seg : (head + 1) * seg] * SCALE
        dq_ref[:, head * HD : (head + 1) * HD] = block.T.astype(BF16)


def weight_kernel(place_ref, x_ref, *refs):
    trees = x_ref.shape[0]
    values, outs = refs[:trees], refs[trees:]
    rows = outs[0].shape[0]
    nx, ny = trees // 2, len(outs)
    px, pc, py = place_ref[0], place_ref[1], place_ref[2]
    for ahead in range(ny):
        part = lax.rem(py + ahead, ny)
        span = pl.ds(pl.multiple_of(part * rows, rows), rows)
        total = None
        for back in range(nx):
            line = 2 * lax.rem(px + nx - back, nx)
            x2 = jnp.concatenate([x_ref[line + pc, span, :], x_ref[line + 1 - pc, span, :]], axis=1)
            v2 = jnp.concatenate([values[2 * back][...], values[2 * back + 1][...]], axis=0)
            term = jnp.dot(x2, v2, preferred_element_type=F32)
            total = term if total is None else total + term
        outs[ahead][...] = total.astype(BF16)


def shift(block, axis, step):
    n = lax.axis_size(axis)
    return lax.ppermute(block, axis, [(i, (i + step) % n) for i in range(n)])


def after(block, *others):
    return lax.optimization_barrier((block, *others))[0]


def plus(a, b):
    return (a.astype(F32) + b.astype(F32)).astype(BF16)


def on_device(queries, keys, values, out_grad, inputs, parents, lengths):
    ny, nx, nc, nz = (lax.axis_size(axis) for axis in ("y", "x", "core", "leaf"))
    seg, features = inputs.shape[1:]
    kv_width, q_width = keys.shape[2], queries.shape[2]
    heads_kv = kv_width // HD
    per_head = q_width // heads_kv
    width = per_head // HD * seg
    rows = nz * seg
    own = lax.axis_index("leaf").astype(jnp.int32).reshape(1)
    scalars = (own, parents[0], lengths[0])

    value_all = lax.all_gather(values[0], "leaf", axis=0, tiled=True)

    group = nx * nc
    owned = features // (ny * group)
    turned = inputs[0].T.reshape(ny, group, owned, seg).transpose(1, 0, 2, 3)
    turned = turned.reshape(group, ny * owned, seg)
    turned = lax.all_to_all(turned, ("x", "core"), 0, 0, tiled=True)

    half = nz // 2
    key_back = [keys[0]] + [None] * (nz - 1)
    for hop in range(1, half + 1):
        held = key_back[hop - 1]
        key_back[hop] = shift(held, "leaf", 1)
        if hop < half:
            key_back[nz - hop] = shift(key_back[(nz - hop + 1) % nz], "leaf", -1)

    turned, *key_back = lax.optimization_barrier((turned, *key_back))

    spec_q = pl.BlockSpec((seg, per_head), lambda k, *_: (0, k))
    spec_b = pl.BlockSpec((seg, HD), lambda k, *_: (0, k))
    spec_k = pl.BlockSpec((rows, HD), lambda k, *_: (0, k))
    spec_s = pl.BlockSpec((1, 1, width), lambda k, *_: (k, 0, 0))
    stats = jax.ShapeDtypeStruct((heads_kv, 1, width), F32)
    stacked = [pltpu.VMEM((width, HD), BF16), pltpu.VMEM((width, HD), BF16)]
    tall = pltpu.VMEM((nz // 2, 2 * seg, width), F32)
    tree = [pltpu.SMEM((nz,), jnp.int32), pltpu.SMEM((nz,), jnp.int32)]
    *value_back, row_max, row_rate = pl.pallas_call(
        value_kernel,
        out_shape=[jax.ShapeDtypeStruct((seg, kv_width), BF16)] * nz + [stats, stats],
        grid_spec=pltpu.PrefetchScalarGridSpec(
            num_scalar_prefetch=3,
            grid=(heads_kv,),
            in_specs=[spec_q, spec_q] + [spec_b] * nz,
            out_specs=[spec_b] * nz + [spec_s, spec_s],
            scratch_shapes=[
                *stacked,
                pltpu.VMEM((nz, seg, HD), BF16),
                pltpu.VMEM((nz, seg, HD), BF16),
                tall,
                pltpu.VMEM((2 * seg, width), BF16),
                *tree,
            ],
        ),
        compiler_params=LIMIT,
        cost_estimate=pl.CostEstimate(
            flops=4 * seg * rows * q_width, bytes_accessed=4 * seg * q_width, transcendentals=0
        ),
    )(*scalars, queries[0], out_grad[0], *key_back)

    def score_grads(first, heads, row_max, kept):
        def moved(spec):
            return pl.BlockSpec(spec.block_shape, lambda k, *_: spec.index_map(k + first))

        given = [moved(spec_q)] * 2 + [moved(spec_s)] * 2 + [moved(spec_b)] * nz + [moved(spec_k)]
        count = len(scalars) + len(given)
        return pl.pallas_call(
            functools.partial(score_kernel, len(kept)),
            out_shape=(
                jax.ShapeDtypeStruct((seg, q_width), BF16),
                jax.ShapeDtypeStruct((rows, kv_width), BF16),
            ),
            grid_spec=pltpu.PrefetchScalarGridSpec(
                num_scalar_prefetch=3,
                grid=(heads,),
                in_specs=given + [pl.BlockSpec(memory_space=pl.ANY)] * len(kept),
                out_specs=[moved(spec_q), moved(spec_k)],
                scratch_shapes=[
                    *stacked,
                    pltpu.VMEM((nz, seg, HD), BF16),
                    tall,
                    tall,
                    pltpu.VMEM((2 * seg, width), BF16),
                    pltpu.VMEM((1, width), F32),
                    pltpu.VMEM((HD, width), F32),
                    *tree,
                ],
            ),
            input_output_aliases={count + i: i for i in range(len(kept))},
            compiler_params=LIMIT,
            cost_estimate=pl.CostEstimate(
                flops=8 * seg * rows * q_width * heads // heads_kv,
                bytes_accessed=6 * seg * q_width * heads // heads_kv,
                transcendentals=0,
            ),
        )(*scalars, queries[0], out_grad[0], row_max, row_rate, *key_back, value_all, *kept)

    up, down = value_back[half], value_back[half - 1]
    grads = ()
    done = 0
    for hop in range(1, half + 1):
        ready = up
        up = shift(up, "leaf", 1)
        if hop < half:
            down = shift(down, "leaf", -1)
        if hop in (2, 3):
            part = heads_kv // 2
            grads = score_grads(done, part, after(row_max, ready), grads)
            done += part
            up, *grads = lax.optimization_barrier((up, *grads))
        if hop < half:
            up = plus(up, value_back[half + hop])
            if hop < half - 1:
                down = plus(down, value_back[half - 1 - hop])
    query_grad, key_part = grads
    value_grad = (
        up.astype(F32) + down.astype(F32) + value_back[0].astype(F32)
    ).astype(BF16)
    key_grad = lax.psum_scatter(key_part, "leaf", scatter_dimension=0, tiled=True)

    line = [value_grad] + [shift(value_grad, "x", back) for back in range(1, nx)]
    both = [block for mine in line for block in (mine, shift(mine, "core", 1))]
    place = jnp.stack([lax.axis_index(axis).astype(jnp.int32) for axis in ("x", "core", "y")])
    whole = pl.BlockSpec(memory_space=pltpu.VMEM)
    terms = pl.pallas_call(
        weight_kernel,
        out_shape=[jax.ShapeDtypeStruct((owned, kv_width), BF16)] * ny,
        in_specs=[pl.BlockSpec(memory_space=pltpu.SMEM)] + [whole] * (1 + group),
        out_specs=[whole] * ny,
        compiler_params=pltpu.CompilerParams(vmem_limit_bytes=24 * 1024 * 1024),
        cost_estimate=pl.CostEstimate(
            flops=2 * features * seg * kv_width, bytes_accessed=4 * features * seg, transcendentals=0
        ),
    )(place, turned, *both)
    term = terms[0].astype(F32)
    for ahead in range(1, ny):
        term = term + shift(terms[ahead], "y", ahead).astype(F32)
    term = term.astype(BF16).reshape(nz, owned // nz, kv_width)
    term = lax.all_to_all(term, "leaf", 0, 0, tiled=True)
    weight_grad = jnp.sum(term.astype(F32), axis=0)
    return (query_grad[None], key_grad[None], value_grad[None], weight_grad)


def solution(mesh):
    trees, nodes = mesh.devices.shape
    side = math.isqrt(trees // 2)
    fine = Mesh(mesh.devices.reshape(side, side, 2, nodes), ("y", "x", "core", "leaf"))
    batch = ("y", "x", "core")
    rows = P(batch, "leaf", None)
    return jax.shard_map(
        on_device,
        mesh=fine,
        in_specs=(rows, rows, rows, rows, rows, P(batch, None), P(batch, None)),
        out_specs=(rows, rows, rows, P((*batch, "leaf"), None)),
        check_vma=False,
    )
```

```python
import functools
import math

import jax
import jax.numpy as jnp
from jax import lax
from jax.experimental import pallas as pl
from jax.experimental.pallas import tpu as pltpu
from jax.sharding import Mesh
from jax.sharding import PartitionSpec as P

HD = 128
NEG = -1e30
TINY = 1e-30
FAR = 1 << 20
TILE = 16
F32 = jnp.float32
BF16 = jnp.bfloat16
NT = (((1,), (1,)), ((), ()))
TN = (((0,), (0,)), ((), ()))
SCALE = 1.0 / math.sqrt(HD)
RATE = SCALE * math.log2(math.e)
LIMIT = pltpu.CompilerParams(vmem_limit_bytes=60 * 1024 * 1024)


def climb(own_ref, par_ref, len_ref, slot_ref, lim_ref, off_ref, nodes):
    own = own_ref[0]
    slot_ref[0] = own
    lim_ref[0] = len_ref[own]
    off_ref[0] = 0
    cursor = own
    count = jnp.int32(1)
    total = tiled(len_ref[own])
    for step in range(1, nodes):
        more = cursor > 0
        up = jnp.where(more, par_ref[cursor], 0)
        length = jnp.where(more, len_ref[up], 0)
        slot_ref[step] = up
        lim_ref[step] = length
        off_ref[step] = total
        total = total + tiled(length)
        count = count + more.astype(jnp.int32)
        cursor = up
    return count, total


def tiled(length):
    return (length + (TILE - 1)) // TILE * TILE


def at(start, size):
    return pl.ds(pl.multiple_of(start, TILE), size)


def each_slot(count, nodes, act):
    for slot in range(nodes):
        pl.when(slot < count)(functools.partial(act, slot))


def stack_heads(q_ref, g_ref, qs, gs, length):
    seg = q_ref.shape[0]
    step = tiled(length)
    live = lax.broadcasted_iota(jnp.int32, (seg, HD), 0) < length
    for head in range(q_ref.shape[1] // HD):
        rows, cols = at(head * step, seg), slice(head * HD, (head + 1) * HD)
        qs[rows, :] = q_ref[:, cols]
        gs[rows, :] = jnp.where(live, g_ref[:, cols], jnp.zeros((), BF16))


def query_places(length, heads, width):
    lane = lax.broadcasted_iota(jnp.int32, (1, width), 1)
    step = tiled(length)
    place = lane
    for head in range(1, heads):
        place = jnp.where(lane >= head * step, lane - head * step, place)
    return place


def first_places(first_ref, lim_ref, off_ref, count, seg, nodes):
    first_ref[...] = jnp.full_like(first_ref, FAR)
    place = lax.broadcasted_iota(jnp.int32, (seg, HD), 0)

    def act(slot):
        seen = place if slot == 0 else jnp.zeros_like(place)
        first_ref[at(off_ref[slot], seg), :] = jnp.where(place < lim_ref[slot], seen, FAR)

    each_slot(count, nodes, act)


def masked_scores(keys, q, first, place):
    s = lax.dot_general(keys, q, NT, preferred_element_type=F32)
    seen = jnp.concatenate([first <= place[:, :HD], first <= place[:, HD:]], axis=1)
    return jnp.where(seen, s, NEG)


def value_kernel(own_ref, par_ref, len_ref, q_ref, g_ref, *refs):
    nodes = (len(refs) - 15) // 2
    keys, values = refs[:nodes], refs[nodes : 2 * nodes]
    t_ref, qs, gs, kc, dvc, kp, first_ref, e_scr, p_low, top_scr, m_scr, l_scr, slot_ref, lim_ref, off_ref = refs[2 * nodes :]
    seg = q_ref.shape[0]
    width = qs.shape[0]
    heads = width // seg
    chunk = 2 * seg
    own = own_ref[0]
    length = len_ref[own]
    count, total = climb(own_ref, par_ref, len_ref, slot_ref, lim_ref, off_ref, nodes)
    pairs = (total + chunk - 1) // chunk

    @pl.when(pl.program_id(0) == 0)
    def _():
        first_places(first_ref, lim_ref, off_ref, count, seg, nodes)
        qs[...] = jnp.zeros_like(qs)
        gs[...] = jnp.zeros_like(gs)
        kp[...] = jnp.zeros_like(kp)

    stack_heads(q_ref, g_ref, qs, gs, length)
    for back in range(nodes):
        kc[back] = keys[back][...]

    def pack(slot):
        kp[at(off_ref[slot], seg), :] = kc[own - slot_ref[slot]]

    each_slot(count, nodes, pack)
    dvc[...] = jnp.zeros_like(dvc)
    m_scr[...] = jnp.full_like(m_scr, NEG)
    l_scr[...] = jnp.zeros_like(l_scr)

    def work(chunks):
        span = chunks * chunk
        place = query_places(length, heads, width)

        def score_step(p, carry):
            rows = at(p * chunk, chunk)
            k2, first = kp[rows, :], first_ref[rows, :]
            for c in range(chunks):
                cols = slice(c * chunk, (c + 1) * chunk)
                s = masked_scores(k2, qs[cols, :], first, place[:, cols])
                before = m_scr[:, cols]
                top = jnp.maximum(before, jnp.max(s, axis=0, keepdims=True))
                e = jnp.exp2((s - top) * RATE)
                e_scr[p, :, cols] = e
                kept = l_scr[:, cols] * jnp.exp2((before - top) * RATE)
                l_scr[:, cols] = kept + jnp.sum(e, axis=0, keepdims=True)
                m_scr[:, cols] = top
                top_scr[p, :, cols] = top
            return carry

        lax.fori_loop(0, pairs, score_step, 0)

        def value_step(p, carry):
            for c in range(chunks):
                cols = slice(c * chunk, (c + 1) * chunk)
                rate = jnp.exp2((top_scr[p, :, cols] - m_scr[:, cols]) * RATE) / l_scr[:, cols]
                p_low[:, cols] = (e_scr[p, :, cols] * rate).astype(BF16)
            dv = jnp.dot(p_low[:, :span], gs[:span, :], preferred_element_type=F32)
            kp[at(p * chunk, chunk), :] = dv.astype(BF16)
            return carry

        lax.fori_loop(0, pairs, value_step, 0)

    for chunks in range(1, width // chunk + 1):
        pl.when((heads * tiled(length) + chunk - 1) // chunk == chunks)(
            functools.partial(work, chunks)
        )
    t_ref[0] = m_scr[...] * RATE + jnp.log2(jnp.maximum(l_scr[...], TINY))
    row = lax.broadcasted_iota(jnp.int32, (seg, HD), 0)

    def unpack(slot):
        dv = kp[at(off_ref[slot], seg), :]
        dvc[own - slot_ref[slot]] = jnp.where(row < lim_ref[slot], dv, jnp.zeros((), BF16))

    each_slot(count, nodes, unpack)
    for back in range(nodes):
        values[back][...] = dvc[back]


def score_kernel(own_ref, par_ref, len_ref, q_ref, g_ref, t_ref, *refs):
    nodes = len(refs) - 19
    keys = refs[:nodes]
    v_ref, dq_ref, dk_ref, qs, gs, kc, kp, vp, dkp, first_ref, s_scr, dp_scr, ds_low, t_scr, dqt, turned, slot_ref, lim_ref, off_ref = refs[nodes:]
    seg = q_ref.shape[0]
    width = qs.shape[0]
    heads = width // seg
    chunk = 2 * seg
    own = own_ref[0]
    length = len_ref[own]
    count, total = climb(own_ref, par_ref, len_ref, slot_ref, lim_ref, off_ref, nodes)
    pairs = (total + chunk - 1) // chunk

    @pl.when(pl.program_id(0) == 0)
    def _():
        first_places(first_ref, lim_ref, off_ref, count, seg, nodes)
        qs[...] = jnp.zeros_like(qs)
        gs[...] = jnp.zeros_like(gs)
        kp[...] = jnp.zeros_like(kp)
        vp[...] = jnp.zeros_like(vp)

    stack_heads(q_ref, g_ref, qs, gs, length)
    for back in range(nodes):
        kc[back] = keys[back][...]

    def whole(slot):
        return pl.ds(pl.multiple_of(slot_ref[slot] * seg, seg), seg)

    def pack(slot):
        kp[at(off_ref[slot], seg), :] = kc[own - slot_ref[slot]]
        vp[at(off_ref[slot], seg), :] = v_ref[whole(slot), :]

    each_slot(count, nodes, pack)
    dk_ref[...] = jnp.zeros_like(dk_ref)
    t_scr[...] = jnp.zeros_like(t_scr)
    dqt[...] = jnp.zeros_like(dqt)

    def work(chunks):
        span = chunks * chunk
        place = query_places(length, heads, width)

        def prob_step(p, carry):
            rows = at(p * chunk, chunk)
            k2, v2, first = kp[rows, :], vp[rows, :], first_ref[rows, :]
            for c in range(chunks):
                cols = slice(c * chunk, (c + 1) * chunk)
                s = masked_scores(k2, qs[cols, :], first, place[:, cols])
                prob = jnp.exp2(s * RATE - t_ref[0, :, cols])
                dp = lax.dot_general(v2, gs[cols, :], NT, preferred_element_type=F32)
                s_scr[p, :, cols] = prob
                dp_scr[p, :, cols] = dp
                t_scr[:, cols] = t_scr[:, cols] + jnp.sum(prob * dp, axis=0, keepdims=True)
            return carry

        lax.fori_loop(0, pairs, prob_step, 0)

        def grad_step(p, carry):
            rows = at(p * chunk, chunk)
            k2 = kp[rows, :]
            for c in range(chunks):
                cols = slice(c * chunk, (c + 1) * chunk)
                ds = (s_scr[p, :, cols] * (dp_scr[p, :, cols] - t_scr[:, cols])).astype(BF16)
                ds_low[:, cols] = ds
                dqt[:, cols] = dqt[:, cols] + lax.dot_general(
                    k2, ds, TN, preferred_element_type=F32
                )
            dk = jnp.dot(ds_low[:, :span], qs[:span, :], preferred_element_type=F32) * SCALE
            dkp[rows, :] = dk.astype(BF16)
            return carry

        lax.fori_loop(0, pairs, grad_step, 0)

    for chunks in range(1, width // chunk + 1):
        pl.when((heads * tiled(length) + chunk - 1) // chunk == chunks)(
            functools.partial(work, chunks)
        )
    row = lax.broadcasted_iota(jnp.int32, (seg, HD), 0)

    def unpack(slot):
        dk = dkp[at(off_ref[slot], seg), :]
        dk_ref[whole(slot), :] = jnp.where(row < lim_ref[slot], dk, jnp.zeros((), BF16))

    each_slot(count, nodes, unpack)
    for part in range(heads):
        turned[part * seg : (part + 1) * seg, :] = dqt[:, part * seg : (part + 1) * seg].T * SCALE
    for head in range(heads):
        dq = turned[at(head * tiled(length), seg), :]
        dq_ref[:, head * HD : (head + 1) * HD] = jnp.where(row < length, dq, 0.0).astype(BF16)


def weight_kernel(place_ref, x_ref, *refs):
    trees = x_ref.shape[0]
    values, outs = refs[:trees], refs[trees:]
    rows = outs[0].shape[0]
    nx, ny = trees // 2, len(outs)
    px, pc, py = place_ref[0], place_ref[1], place_ref[2]
    for ahead in range(ny):
        part = lax.rem(py + ahead, ny)
        span = pl.ds(pl.multiple_of(part * rows, rows), rows)
        total = None
        for back in range(nx):
            line = 2 * lax.rem(px + nx - back, nx)
            x2 = jnp.concatenate([x_ref[line + pc, span, :], x_ref[line + 1 - pc, span, :]], axis=1)
            v2 = jnp.concatenate([values[2 * back][...], values[2 * back + 1][...]], axis=0)
            term = jnp.dot(x2, v2, preferred_element_type=F32)
            total = term if total is None else total + term
        outs[ahead][...] = total.astype(BF16)


def shift(block, axis, step):
    n = lax.axis_size(axis)
    return lax.ppermute(block, axis, [(i, (i + step) % n) for i in range(n)])


def after(block, *others):
    return lax.optimization_barrier((block, *others))[0]


def plus(a, b):
    return (a.astype(F32) + b.astype(F32)).astype(BF16)


def on_device(queries, keys, values, out_grad, inputs, parents, lengths):
    ny, nx, nc, nz = (lax.axis_size(axis) for axis in ("y", "x", "core", "leaf"))
    seg, features = inputs.shape[1:]
    kv_width, q_width = keys.shape[2], queries.shape[2]
    heads_kv = kv_width // HD
    per_head = q_width // heads_kv
    width = per_head // HD * seg
    rows = nz * seg
    own = lax.axis_index("leaf").astype(jnp.int32).reshape(1)
    scalars = (own, parents[0], lengths[0])

    value_all = lax.all_gather(values[0], "leaf", axis=0, tiled=True)

    group = nx * nc
    owned = features // (ny * group)
    facing = inputs[0].T.reshape(ny, group, owned, seg).transpose(1, 0, 2, 3)
    facing = facing.reshape(group, ny * owned, seg)

    half = nz // 2
    key_back = [keys[0]] + [None] * (nz - 1)
    for hop in range(1, half + 1):
        held = key_back[hop - 1]
        if hop == 2:
            held = after(held, facing)
        key_back[hop] = shift(held, "leaf", 1)
        if hop == 1:
            turned = lax.all_to_all(after(facing, key_back[1]), ("x", "core"), 0, 0, tiled=True)
        if hop < half:
            key_back[nz - hop] = shift(key_back[(nz - hop + 1) % nz], "leaf", -1)

    spec_q = pl.BlockSpec((seg, per_head), lambda k, *_: (0, k))
    spec_b = pl.BlockSpec((seg, HD), lambda k, *_: (0, k))
    spec_k = pl.BlockSpec((rows, HD), lambda k, *_: (0, k))
    spec_s = pl.BlockSpec((1, 1, width), lambda k, *_: (k, 0, 0))
    stats = jax.ShapeDtypeStruct((heads_kv, 1, width), F32)
    stacked = [pltpu.VMEM((width, HD), BF16), pltpu.VMEM((width, HD), BF16)]
    tall = pltpu.VMEM((nz // 2, 2 * seg, width), F32)
    tree = [pltpu.SMEM((nz,), jnp.int32)] * 3
    packed = pltpu.VMEM((rows, HD), BF16)
    places = pltpu.VMEM((rows, HD), jnp.int32)
    *value_back, row_log = pl.pallas_call(
        value_kernel,
        out_shape=[jax.ShapeDtypeStruct((seg, kv_width), BF16)] * nz + [stats],
        grid_spec=pltpu.PrefetchScalarGridSpec(
            num_scalar_prefetch=3,
            grid=(heads_kv,),
            in_specs=[spec_q, spec_q] + [spec_b] * nz,
            out_specs=[spec_b] * nz + [spec_s],
            scratch_shapes=[
                *stacked,
                pltpu.VMEM((nz, seg, HD), BF16),
                pltpu.VMEM((nz, seg, HD), BF16),
                packed,
                places,
                tall,
                pltpu.VMEM((2 * seg, width), BF16),
                pltpu.VMEM((nz // 2, 1, width), F32),
                pltpu.VMEM((1, width), F32),
                pltpu.VMEM((1, width), F32),
                *tree,
            ],
        ),
        compiler_params=LIMIT,
        cost_estimate=pl.CostEstimate(
            flops=4 * seg * rows * q_width, bytes_accessed=4 * seg * q_width, transcendentals=0
        ),
    )(*scalars, queries[0], out_grad[0], *key_back)

    def score_grads(row_log):
        return pl.pallas_call(
            score_kernel,
            out_shape=(
                jax.ShapeDtypeStruct((seg, q_width), BF16),
                jax.ShapeDtypeStruct((rows, kv_width), BF16),
            ),
            grid_spec=pltpu.PrefetchScalarGridSpec(
                num_scalar_prefetch=3,
                grid=(heads_kv,),
                in_specs=[spec_q, spec_q, spec_s] + [spec_b] * nz + [spec_k],
                out_specs=[spec_q, spec_k],
                scratch_shapes=[
                    *stacked,
                    pltpu.VMEM((nz, seg, HD), BF16),
                    packed,
                    packed,
                    packed,
                    places,
                    tall,
                    tall,
                    pltpu.VMEM((2 * seg, width), BF16),
                    pltpu.VMEM((1, width), F32),
                    pltpu.VMEM((HD, width), F32),
                    pltpu.VMEM((width, HD), F32),
                    *tree,
                ],
            ),
            compiler_params=LIMIT,
            cost_estimate=pl.CostEstimate(
                flops=8 * seg * rows * q_width, bytes_accessed=6 * seg * q_width, transcendentals=0
            ),
        )(*scalars, queries[0], out_grad[0], row_log, *key_back, value_all)

    up, down = value_back[half], value_back[half - 1]
    for hop in range(1, half + 1):
        ready = up
        up = shift(up, "leaf", 1)
        if hop < half:
            down = shift(down, "leaf", -1)
        if hop == 2:
            query_grad, key_part = score_grads(after(row_log, ready))
            up, query_grad, key_part, turned = lax.optimization_barrier(
                (up, query_grad, key_part, turned)
            )
        if hop < half:
            up = plus(up, value_back[half + hop])
            if hop < half - 1:
                down = plus(down, value_back[half - 1 - hop])
    value_grad = (
        up.astype(F32) + down.astype(F32) + value_back[0].astype(F32)
    ).astype(BF16)
    key_grad = lax.psum_scatter(key_part, "leaf", scatter_dimension=0, tiled=True)

    line = [value_grad] + [shift(value_grad, "x", back) for back in range(1, nx)]
    both = [block for mine in line for block in (mine, shift(mine, "core", 1))]
    place = jnp.stack([lax.axis_index(axis).astype(jnp.int32) for axis in ("x", "core", "y")])
    whole = pl.BlockSpec(memory_space=pltpu.VMEM)
    terms = pl.pallas_call(
        weight_kernel,
        out_shape=[jax.ShapeDtypeStruct((owned, kv_width), BF16)] * ny,
        in_specs=[pl.BlockSpec(memory_space=pltpu.SMEM)] + [whole] * (1 + group),
        out_specs=[whole] * ny,
        compiler_params=pltpu.CompilerParams(vmem_limit_bytes=24 * 1024 * 1024),
        cost_estimate=pl.CostEstimate(
            flops=2 * features * seg * kv_width, bytes_accessed=4 * features * seg, transcendentals=0
        ),
    )(place, turned, *both)
    term = terms[0].astype(F32)
    for ahead in range(1, ny):
        term = term + shift(terms[ahead], "y", ahead).astype(F32)
    term = term.astype(BF16).reshape(nz, owned // nz, kv_width)
    term = lax.all_to_all(term, "leaf", 0, 0, tiled=True)
    weight_grad = jnp.sum(term.astype(F32), axis=0)
    return (query_grad[None], key_grad[None], value_grad[None], weight_grad)


def solution(mesh):
    trees, nodes = mesh.devices.shape
    side = math.isqrt(trees // 2)
    fine = Mesh(mesh.devices.reshape(side, side, 2, nodes), ("y", "x", "core", "leaf"))
    batch = ("y", "x", "core")
    rows = P(batch, "leaf", None)
    return jax.shard_map(
        on_device,
        mesh=fine,
        in_specs=(rows, rows, rows, rows, rows, P(batch, None), P(batch, None)),
        out_specs=(rows, rows, rows, P((*batch, "leaf"), None)),
        check_vma=False,
    )
```

```python
import functools
import math

import jax
import jax.numpy as jnp
from jax import lax
from jax.experimental import pallas as pl
from jax.experimental.pallas import tpu as pltpu
from jax.sharding import Mesh
from jax.sharding import PartitionSpec as P

HD = 128
NEG = -1e30
TINY = 1e-30
FAR = 1 << 20
TILE = 16
F32 = jnp.float32
BF16 = jnp.bfloat16
NT = (((1,), (1,)), ((), ()))
TN = (((0,), (0,)), ((), ()))
SCALE = 1.0 / math.sqrt(HD)
RATE = SCALE * math.log2(math.e)
LIMIT = pltpu.CompilerParams(vmem_limit_bytes=60 * 1024 * 1024)


def climb(own_ref, par_ref, len_ref, lim_ref, off_ref, nodes):
    own = own_ref[0]
    for back in range(nodes):
        lim_ref[back] = 0
        off_ref[back] = 0
    lim_ref[0] = len_ref[own]
    total = tiled(len_ref[own])
    cursor = own
    for _ in range(1, nodes):
        more = cursor > 0
        up = jnp.where(more, par_ref[cursor], 0)
        length = len_ref[up]
        back = own - up

        @pl.when(more)
        def _(back=back, length=length, total=total):
            lim_ref[back] = length
            off_ref[back] = total

        total = total + jnp.where(more, tiled(length), 0)
        cursor = up
    return total


def tiled(length):
    return (length + (TILE - 1)) // TILE * TILE


def at(start, size):
    return pl.ds(pl.multiple_of(start, TILE), size)


def each_member(lim_ref, nodes, act):
    for back in range(nodes):
        pl.when(lim_ref[back] > 0)(functools.partial(act, back))


def stack_heads(q_ref, g_ref, qs, gs, length):
    seg = q_ref.shape[0]
    step = tiled(length)
    live = lax.broadcasted_iota(jnp.int32, (seg, HD), 0) < length
    for head in range(q_ref.shape[1] // HD):
        rows, cols = at(head * step, seg), slice(head * HD, (head + 1) * HD)
        qs[rows, :] = q_ref[:, cols]
        gs[rows, :] = jnp.where(live, g_ref[:, cols], jnp.zeros((), BF16))


def query_places(length, heads, width):
    lane = lax.broadcasted_iota(jnp.int32, (1, width), 1)
    step = tiled(length)
    place = lane
    for head in range(1, heads):
        place = jnp.where(lane >= head * step, lane - head * step, place)
    return place


def first_places(first_ref, lim_ref, off_ref, seg, nodes):
    first_ref[...] = jnp.full_like(first_ref, FAR)
    place = lax.broadcasted_iota(jnp.int32, (seg, HD), 0)

    def act(back):
        seen = place if back == 0 else jnp.zeros_like(place)
        first_ref[at(off_ref[back], seg), :] = jnp.where(place < lim_ref[back], seen, FAR)

    each_member(lim_ref, nodes, act)


def masked_scores(keys, q, first, place):
    s = lax.dot_general(keys, q, NT, preferred_element_type=F32)
    seen = jnp.concatenate([first <= place[:, :HD], first <= place[:, HD:]], axis=1)
    return jnp.where(seen, s, NEG)


def value_kernel(own_ref, par_ref, len_ref, q_ref, g_ref, *refs):
    nodes = (len(refs) - 12) // 2
    keys, values = refs[:nodes], refs[nodes : 2 * nodes]
    t_ref, qs, gs, kp, first_ref, e_scr, p_low, top_scr, m_scr, l_scr, lim_ref, off_ref = refs[2 * nodes :]
    seg = q_ref.shape[0]
    width = qs.shape[0]
    heads = width // seg
    chunk = 2 * seg
    own = own_ref[0]
    length = len_ref[own]
    total = climb(own_ref, par_ref, len_ref, lim_ref, off_ref, nodes)
    pairs = (total + chunk - 1) // chunk

    @pl.when(pl.program_id(0) == 0)
    def _():
        first_places(first_ref, lim_ref, off_ref, seg, nodes)
        qs[...] = jnp.zeros_like(qs)
        gs[...] = jnp.zeros_like(gs)
        kp[...] = jnp.zeros_like(kp)

    stack_heads(q_ref, g_ref, qs, gs, length)

    def pack(back):
        kp[at(off_ref[back], seg), :] = keys[back][...]

    each_member(lim_ref, nodes, pack)
    m_scr[...] = jnp.full_like(m_scr, NEG)
    l_scr[...] = jnp.zeros_like(l_scr)

    def work(chunks):
        span = chunks * chunk
        place = query_places(length, heads, width)

        def score_step(p, carry):
            rows = at(p * chunk, chunk)
            k2, first = kp[rows, :], first_ref[rows, :]
            for c in range(chunks):
                cols = slice(c * chunk, (c + 1) * chunk)
                s = masked_scores(k2, qs[cols, :], first, place[:, cols])
                before = m_scr[:, cols]
                top = jnp.maximum(before, jnp.max(s, axis=0, keepdims=True))
                e = jnp.exp2((s - top) * RATE)
                e_scr[p, :, cols] = e
                kept = l_scr[:, cols] * jnp.exp2((before - top) * RATE)
                l_scr[:, cols] = kept + jnp.sum(e, axis=0, keepdims=True)
                m_scr[:, cols] = top
                top_scr[p, :, cols] = top
            return carry

        lax.fori_loop(0, pairs, score_step, 0)

        def value_step(p, carry):
            for c in range(chunks):
                cols = slice(c * chunk, (c + 1) * chunk)
                rate = jnp.exp2((top_scr[p, :, cols] - m_scr[:, cols]) * RATE) / l_scr[:, cols]
                p_low[:, cols] = (e_scr[p, :, cols] * rate).astype(BF16)
            dv = jnp.dot(p_low[:, :span], gs[:span, :], preferred_element_type=F32)
            kp[at(p * chunk, chunk), :] = dv.astype(BF16)
            return carry

        lax.fori_loop(0, pairs, value_step, 0)

    for chunks in range(1, width // chunk + 1):
        pl.when((heads * tiled(length) + chunk - 1) // chunk == chunks)(
            functools.partial(work, chunks)
        )
    t_ref[0] = m_scr[...] * RATE + jnp.log2(jnp.maximum(l_scr[...], TINY))
    row = lax.broadcasted_iota(jnp.int32, (seg, HD), 0)

    for back in range(nodes):
        dv = kp[at(off_ref[back], seg), :]
        values[back][...] = jnp.where(row < lim_ref[back], dv, jnp.zeros((), BF16))


def score_kernel(kept, own_ref, par_ref, len_ref, q_ref, g_ref, t_ref, *refs):
    nodes = len(refs) - 17 - kept
    keys = refs[:nodes]
    v_ref = refs[nodes]
    dq_ref, dk_ref, qs, gs, kp, vp, dkp, first_ref, s_scr, dp_scr, ds_low, t_scr, dqt, turned, lim_ref, off_ref = refs[nodes + 1 + kept :]
    seg = q_ref.shape[0]
    width = qs.shape[0]
    heads = width // seg
    chunk = 2 * seg
    own = own_ref[0]
    length = len_ref[own]
    total = climb(own_ref, par_ref, len_ref, lim_ref, off_ref, nodes)
    pairs = (total + chunk - 1) // chunk

    @pl.when(pl.program_id(0) == 0)
    def _():
        first_places(first_ref, lim_ref, off_ref, seg, nodes)
        qs[...] = jnp.zeros_like(qs)
        gs[...] = jnp.zeros_like(gs)
        kp[...] = jnp.zeros_like(kp)
        vp[...] = jnp.zeros_like(vp)

    stack_heads(q_ref, g_ref, qs, gs, length)

    def whole(back):
        return pl.ds(pl.multiple_of((own - back) * seg, seg), seg)

    def pack(back):
        kp[at(off_ref[back], seg), :] = keys[back][...]
        vp[at(off_ref[back], seg), :] = v_ref[whole(back), :]

    each_member(lim_ref, nodes, pack)
    dk_ref[...] = jnp.zeros_like(dk_ref)
    t_scr[...] = jnp.zeros_like(t_scr)
    dqt[...] = jnp.zeros_like(dqt)

    def work(chunks):
        span = chunks * chunk
        place = query_places(length, heads, width)

        def prob_step(p, carry):
            rows = at(p * chunk, chunk)
            k2, v2, first = kp[rows, :], vp[rows, :], first_ref[rows, :]
            for c in range(chunks):
                cols = slice(c * chunk, (c + 1) * chunk)
                s = masked_scores(k2, qs[cols, :], first, place[:, cols])
                prob = jnp.exp2(s * RATE - t_ref[0, :, cols])
                dp = lax.dot_general(v2, gs[cols, :], NT, preferred_element_type=F32)
                s_scr[p, :, cols] = prob
                dp_scr[p, :, cols] = dp
                t_scr[:, cols] = t_scr[:, cols] + jnp.sum(prob * dp, axis=0, keepdims=True)
            return carry

        lax.fori_loop(0, pairs, prob_step, 0)

        def grad_step(p, carry):
            rows = at(p * chunk, chunk)
            k2 = kp[rows, :]
            for c in range(chunks):
                cols = slice(c * chunk, (c + 1) * chunk)
                ds = (s_scr[p, :, cols] * (dp_scr[p, :, cols] - t_scr[:, cols])).astype(BF16)
                ds_low[:, cols] = ds
                dqt[:, cols] = dqt[:, cols] + lax.dot_general(
                    k2, ds, TN, preferred_element_type=F32
                )
            dk = jnp.dot(ds_low[:, :span], qs[:span, :], preferred_element_type=F32) * SCALE
            dkp[rows, :] = dk.astype(BF16)
            return carry

        lax.fori_loop(0, pairs, grad_step, 0)

    for chunks in range(1, width // chunk + 1):
        pl.when((heads * tiled(length) + chunk - 1) // chunk == chunks)(
            functools.partial(work, chunks)
        )
    row = lax.broadcasted_iota(jnp.int32, (seg, HD), 0)

    def unpack(back):
        dk = dkp[at(off_ref[back], seg), :]
        dk_ref[whole(back), :] = jnp.where(row < lim_ref[back], dk, jnp.zeros((), BF16))

    each_member(lim_ref, nodes, unpack)
    for part in range(heads):
        turned[part * seg : (part + 1) * seg, :] = dqt[:, part * seg : (part + 1) * seg].T * SCALE
    for head in range(heads):
        dq = turned[at(head * tiled(length), seg), :]
        dq_ref[:, head * HD : (head + 1) * HD] = jnp.where(row < length, dq, 0.0).astype(BF16)


def weight_kernel(place_ref, x_ref, *refs):
    trees = x_ref.shape[0]
    values, outs = refs[:trees], refs[trees:]
    rows = outs[0].shape[0]
    nx, ny = trees // 2, len(outs)
    px, pc, py = place_ref[0], place_ref[1], place_ref[2]
    for ahead in range(ny):
        part = lax.rem(py + ahead, ny)
        span = pl.ds(pl.multiple_of(part * rows, rows), rows)
        total = None
        for back in range(nx):
            line = 2 * lax.rem(px + nx - back, nx)
            x2 = jnp.concatenate([x_ref[line + pc, span, :], x_ref[line + 1 - pc, span, :]], axis=1)
            v2 = jnp.concatenate([values[2 * back][...], values[2 * back + 1][...]], axis=0)
            term = jnp.dot(x2, v2, preferred_element_type=F32)
            total = term if total is None else total + term
        outs[ahead][...] = total.astype(BF16)


def shift(block, axis, step):
    n = lax.axis_size(axis)
    return lax.ppermute(block, axis, [(i, (i + step) % n) for i in range(n)])


def after(block, *others):
    return lax.optimization_barrier((block, *others))[0]


def plus(a, b):
    return (a.astype(F32) + b.astype(F32)).astype(BF16)


def on_device(queries, keys, values, out_grad, inputs, parents, lengths):
    ny, nx, nc, nz = (lax.axis_size(axis) for axis in ("y", "x", "core", "leaf"))
    seg, features = inputs.shape[1:]
    kv_width, q_width = keys.shape[2], queries.shape[2]
    heads_kv = kv_width // HD
    per_head = q_width // heads_kv
    width = per_head // HD * seg
    rows = nz * seg
    own = lax.axis_index("leaf").astype(jnp.int32).reshape(1)
    scalars = (own, parents[0], lengths[0])

    value_all = lax.all_gather(values[0], "leaf", axis=0, tiled=True)

    group = nx * nc
    owned = features // (ny * group)
    facing = inputs[0].T.reshape(ny, group, owned, seg).transpose(1, 0, 2, 3)
    facing = facing.reshape(group, ny * owned, seg)

    half = nz // 2
    key_back = [keys[0]] + [None] * (nz - 1)
    for hop in range(1, half + 1):
        held = key_back[hop - 1]
        if hop == 2:
            held = after(held, facing)
        key_back[hop] = shift(held, "leaf", 1)
        if hop == 1:
            turned = lax.all_to_all(after(facing, key_back[1]), ("x", "core"), 0, 0, tiled=True)
        if hop < half:
            key_back[nz - hop] = shift(key_back[(nz - hop + 1) % nz], "leaf", -1)

    spec_q = pl.BlockSpec((seg, per_head), lambda k, *_: (0, k))
    spec_b = pl.BlockSpec((seg, HD), lambda k, *_: (0, k))
    spec_k = pl.BlockSpec((rows, HD), lambda k, *_: (0, k))
    spec_s = pl.BlockSpec((1, 1, width), lambda k, *_: (k, 0, 0))
    stats = jax.ShapeDtypeStruct((heads_kv, 1, width), F32)
    stacked = [pltpu.VMEM((width, HD), BF16), pltpu.VMEM((width, HD), BF16)]
    tall = pltpu.VMEM((nz // 2, 2 * seg, width), F32)
    tree = [pltpu.SMEM((nz,), jnp.int32)] * 2
    packed = pltpu.VMEM((rows, HD), BF16)
    places = pltpu.VMEM((rows, HD), jnp.int32)
    *value_back, row_log = pl.pallas_call(
        value_kernel,
        out_shape=[jax.ShapeDtypeStruct((seg, kv_width), BF16)] * nz + [stats],
        grid_spec=pltpu.PrefetchScalarGridSpec(
            num_scalar_prefetch=3,
            grid=(heads_kv,),
            in_specs=[spec_q, spec_q] + [spec_b] * nz,
            out_specs=[spec_b] * nz + [spec_s],
            scratch_shapes=[
                *stacked,
                packed,
                places,
                tall,
                pltpu.VMEM((2 * seg, width), BF16),
                pltpu.VMEM((nz // 2, 1, width), F32),
                pltpu.VMEM((1, width), F32),
                pltpu.VMEM((1, width), F32),
                *tree,
            ],
        ),
        compiler_params=LIMIT,
        cost_estimate=pl.CostEstimate(
            flops=4 * seg * rows * q_width, bytes_accessed=4 * seg * q_width, transcendentals=0
        ),
    )(*scalars, queries[0], out_grad[0], *key_back)

    def score_grads(first, heads, row_log, kept):
        def moved(spec):
            return pl.BlockSpec(spec.block_shape, lambda k, *_: spec.index_map(k + first))

        given = [moved(spec) for spec in [spec_q, spec_q, spec_s] + [spec_b] * nz + [spec_k]]
        count = len(scalars) + len(given)
        return pl.pallas_call(
            functools.partial(score_kernel, len(kept)),
            out_shape=(
                jax.ShapeDtypeStruct((seg, q_width), BF16),
                jax.ShapeDtypeStruct((rows, kv_width), BF16),
            ),
            grid_spec=pltpu.PrefetchScalarGridSpec(
                num_scalar_prefetch=3,
                grid=(heads,),
                in_specs=given + [pl.BlockSpec(memory_space=pl.ANY)] * len(kept),
                out_specs=[moved(spec_q), moved(spec_k)],
                scratch_shapes=[
                    *stacked,
                    packed,
                    packed,
                    packed,
                    places,
                    tall,
                    tall,
                    pltpu.VMEM((2 * seg, width), BF16),
                    pltpu.VMEM((1, width), F32),
                    pltpu.VMEM((HD, width), F32),
                    pltpu.VMEM((width, HD), F32),
                    *tree,
                ],
            ),
            input_output_aliases={count + i: i for i in range(len(kept))},
            compiler_params=LIMIT,
            cost_estimate=pl.CostEstimate(
                flops=8 * seg * rows * q_width, bytes_accessed=6 * seg * q_width, transcendentals=0
            ),
        )(*scalars, queries[0], out_grad[0], row_log, *key_back, value_all, *kept)

    up, down = value_back[half], value_back[half - 1]
    grads = ()
    for hop in range(1, half + 1):
        ready = up
        up = shift(up, "leaf", 1)
        if hop < half:
            down = shift(down, "leaf", -1)
        if hop in (2, 3):
            part = heads_kv // 2
            grads = score_grads((hop - 2) * part, part, after(row_log, ready), grads)
            up, turned, *grads = lax.optimization_barrier((up, turned, *grads))
        if hop < half:
            up = plus(up, value_back[half + hop])
            if hop < half - 1:
                down = plus(down, value_back[half - 1 - hop])
    query_grad, key_part = grads
    value_grad = (
        up.astype(F32) + down.astype(F32) + value_back[0].astype(F32)
    ).astype(BF16)
    key_grad = lax.psum_scatter(key_part, "leaf", scatter_dimension=0, tiled=True)

    line = [value_grad] + [shift(value_grad, "x", back) for back in range(1, nx)]
    both = [block for mine in line for block in (mine, shift(mine, "core", 1))]
    place = jnp.stack([lax.axis_index(axis).astype(jnp.int32) for axis in ("x", "core", "y")])
    whole = pl.BlockSpec(memory_space=pltpu.VMEM)
    terms = pl.pallas_call(
        weight_kernel,
        out_shape=[jax.ShapeDtypeStruct((owned, kv_width), BF16)] * ny,
        in_specs=[pl.BlockSpec(memory_space=pltpu.SMEM)] + [whole] * (1 + group),
        out_specs=[whole] * ny,
        compiler_params=pltpu.CompilerParams(vmem_limit_bytes=24 * 1024 * 1024),
        cost_estimate=pl.CostEstimate(
            flops=2 * features * seg * kv_width, bytes_accessed=4 * features * seg, transcendentals=0
        ),
    )(place, turned, *both)
    term = terms[0].astype(F32)
    for ahead in range(1, ny):
        term = term + shift(terms[ahead], "y", ahead).astype(F32)
    term = term.astype(BF16).reshape(nz, owned // nz, kv_width)
    term = lax.all_to_all(term, "leaf", 0, 0, tiled=True)
    weight_grad = jnp.sum(term.astype(F32), axis=0)
    return (query_grad[None], key_grad[None], value_grad[None], weight_grad)


def solution(mesh):
    trees, nodes = mesh.devices.shape
    side = math.isqrt(trees // 2)
    fine = Mesh(mesh.devices.reshape(side, side, 2, nodes), ("y", "x", "core", "leaf"))
    batch = ("y", "x", "core")
    rows = P(batch, "leaf", None)
    return jax.shard_map(
        on_device,
        mesh=fine,
        in_specs=(rows, rows, rows, rows, rows, P(batch, None), P(batch, None)),
        out_specs=(rows, rows, rows, P((*batch, "leaf"), None)),
        check_vma=False,
    )
```
